768 devices in a mesh: seq: 96 (over y, z), vocab: 8 (over x, core).
Axes of the slice: x: 4, y: 8, z: 12, core: 2. Of those that a mesh axis runs over, the one named last changes fastest.
Arguments:
- neighbour_ids: int32 [24576], P('seq'), may hold values from 0 to 122879, as said below
- table_cols: bfloat16 [896, 122880], P('vocab', 'seq')
- gain: float32 [896], replicated, may hold values from 0.1 to 1.9
- w_in: bfloat16 [896, 3584], P(None, 'vocab'), may hold values from -0.1875 to 0.1875
- w_out: bfloat16 [3584, 896], P('vocab'), may hold values from -0.09375 to 0.09375
Outputs:
- encoded: bfloat16 [896, 24576], P('vocab', 'seq')
The draws below stay inside these ranges and needn't reach their ends.
Inputs may be any that keep to these rules, and one draw needn't show every extreme that they name: `neighbour_ids`: in each aligned block of 256 entries, at most 6 ids lie in any one range [r * 1280, (r + 1) * 1280); one range, the same for all blocks, holds exactly 6 ids of every block.
All inputs are finite; a program needn't handle non-finite values.
Results may differ from the reference program's by a relative error of at most 0.0052.
Values may be sent and summed in bfloat16 or wider, within the bound.
No kernel may reach another device: no remote copies, remote signals or barrier semaphores. Data moves between devices by JAX's collectives and lax.ppermute only.
A program may use at most 32 MiB of HBM per device.

```python
import jax
import jax.numpy as jnp
from jax import lax

E = 896
FF = 3584
VOC_SEQ = 1280
NEIGH_TOK = 256
VOCAB = 122880
CAP = 6
N_SEQ = 96


def draw_neighbour_ids(key, part):
    key = jax.random.fold_in(key, 7)
    key_hot, key_score, key_order, key_offset = jax.random.split(key, 4)
    slot_total = N_SEQ * CAP
    hot_owner = jax.random.randint(key_hot, (), 0, N_SEQ)
    candidate = jnp.arange(slot_total, dtype=jnp.int32)
    cand_owner = candidate // CAP
    scores = jax.random.randint(key_score, (N_SEQ, slot_total), 0, 1024) * slot_total + candidate[None, :]
    scores = jnp.where(cand_owner[None, :] == hot_owner, candidate[None, :] - slot_total, scores)
    picked = jnp.argsort(scores, axis=1)[:, :NEIGH_TOK]
    owners = picked // CAP
    order_scores = jax.random.randint(key_order, (N_SEQ, NEIGH_TOK), 0, 1024) * NEIGH_TOK + jnp.arange(NEIGH_TOK, dtype=jnp.int32)[None, :]
    order = jnp.argsort(order_scores, axis=1)
    owners = jnp.take_along_axis(owners, order, axis=1)
    offsets = jax.random.randint(key_offset, (N_SEQ, NEIGH_TOK), 0, VOC_SEQ)
    return (owners * VOC_SEQ + offsets).reshape(-1).astype(jnp.int32)


def draw_table_cols(key, part):
    key = jax.random.fold_in(key, 13)
    key_feat, key_row, key_base = jax.random.split(key, 3)
    feat_scale = jnp.exp(jax.random.uniform(key_feat, (E, 1), jnp.float32, jnp.log(0.5), jnp.log(5.0)))
    row_scale = jnp.exp(jax.random.uniform(key_row, (1, VOCAB), jnp.float32, jnp.log(0.1), jnp.log(1.0)))
    values = jax.random.truncated_normal(key_base, -4.0, 4.0, (E, VOCAB), jnp.float32)
    return (0.6 * values * feat_scale * row_scale).astype(jnp.bfloat16)


def steps_of(key, extent, shards, low, top_value):
    def one(dim, shards_of):
        heights = jax.random.uniform(jax.random.fold_in(jax.random.fold_in(key, 6), dim), (shards_of,), jnp.float32, low / len(shards), top_value / len(shards))
        return jnp.repeat(jnp.exp(heights), extent[dim] // shards_of).reshape((-1,) + (1,) * (len(extent) - dim - 1))

    level = one(*shards[0])
    for cut in shards[1:]:
        level = level * one(*cut)
    return level


def normal_values(own_key, dims, width, most, cuts=(), kind=jnp.bfloat16):
    factor_of = steps_of(own_key, dims, cuts, -0.22, 0.18) if cuts else 1.0
    result = jax.random.normal(own_key, dims, jnp.float32) * width * factor_of
    return jnp.minimum(jnp.maximum(result, -most), most).astype(kind)


def setup_inputs(seed: int = 0) -> dict:
    seeds = jax.random.split(jax.random.key(seed), 6)
    neighbour_ids = draw_neighbour_ids(jax.random.fold_in(seeds[5], 71), 0)
    table_cols = draw_table_cols(jax.random.fold_in(seeds[5], 71), 0)
    gain = jnp.clip(1.0 + 0.18 * jax.random.normal(seeds[2], (E,), jnp.float32), 0.1, 1.9)
    w_in = normal_values(seeds[3], (E, FF), E ** -0.5, 0.1875, ((1, 8),))
    w_out = normal_values(seeds[4], (FF, E), FF ** -0.5, 0.09375, ((0, 8),))
    return dict(neighbour_ids=neighbour_ids, table_cols=table_cols, gain=gain, w_in=w_in, w_out=w_out)


norm_eps = 1e-05

def reference(neighbour_ids, table_cols, gain, w_in, w_out):
    embedded = jnp.take(table_cols, neighbour_ids, axis=1)
    widened = embedded.astype(jnp.float32)
    meansq = lax.optimization_barrier(jnp.mean(widened * widened, axis=0))
    scaled = (gain.astype(jnp.float32)[:, None] * widened).astype(jnp.bfloat16)
    pre = jnp.dot(w_in.T, scaled, preferred_element_type=jnp.float32) * lax.rsqrt(meansq + norm_eps)[None, :]
    hidden = jax.nn.gelu(pre, approximate=True).astype(jnp.bfloat16)
    total = jnp.dot(w_out.T, hidden, preferred_element_type=jnp.float32)
    return (widened + total).astype(jnp.bfloat16)
```

```python
import functools

import jax
import jax.numpy as jnp
from jax import lax
from jax.experimental import pallas as pl
from jax.experimental.pallas import tpu as pltpu
from jax.sharding import Mesh, PartitionSpec as P

CAP = 6
SLOTS = 8
SPLIT = 64
NORM_EPS = 1e-05
F32 = jnp.float32
BF16 = jnp.bfloat16
I32 = jnp.int32


def iota(shape, dim):
    return lax.broadcasted_iota(I32, shape, dim)


def hot(mask):
    return jnp.where(mask, 1.0, 0.0).astype(BF16)


def dot(a, b, ca, cb):
    return lax.dot_general(a, b, (((ca,), (cb,)), ((), ())), preferred_element_type=F32)


def request_kernel(rows, ids_ref, out_ref, slot_ref):
    owners, toks = out_ref.shape[0], ids_ref.shape[1]
    ids = ids_ref[...]
    owner = ids // rows
    code = ids - owner * rows + 1
    mine = iota((owners, toks), 0) == owner
    mine_hot = hot(mine)
    earlier = hot(iota((toks, toks), 0) < iota((toks, toks), 1))
    count = dot(mine_hot, earlier, 1, 0)
    rank = jnp.sum(jnp.where(mine, count, 0.0), axis=0, keepdims=True).astype(I32)
    at = iota((SLOTS, toks), 0) == rank
    high = jnp.where(at, code // SPLIT, 0).astype(F32).astype(BF16)
    low = jnp.where(at, code % SPLIT, 0).astype(F32).astype(BF16)
    out = dot(mine_hot, high, 1, 1) * SPLIT + dot(mine_hot, low, 1, 1)
    out_ref[:, 0, :] = out.astype(I32)
    slot_ref[...] = owner * SLOTS + rank


def layer_kernel(block_ref, table_ref, own_ref, gain_ref, in_a, in_b, out_a, out_b,
                 part_ref, emb_ref, pick, scaled, hidden):
    sources = block_ref.shape[0]
    feats, rows = table_ref.shape
    cols = sources * CAP
    code = block_ref[:, 0, :]
    spread = hot(iota((sources, cols), 1) // CAP == iota((sources, cols), 0))
    high = (code // SPLIT).astype(F32).astype(BF16)
    low = (code % SPLIT).astype(F32).astype(BF16)
    wide = dot(high, spread, 0, 0) * SPLIT + dot(low, spread, 0, 0)
    lane = iota((SLOTS, cols), 1)
    local = jnp.sum(jnp.where(lane - (lane // CAP) * CAP == iota((SLOTS, cols), 0), wide, 0.0), axis=0, keepdims=True)
    local = local.astype(I32) - 1
    pick[...] = hot(iota((rows, cols), 0) == local)
    emb_ref[...] = dot(own_ref[...], pick[...], 1, 0).astype(BF16)
    squares = jnp.zeros((1, cols), F32)
    step = feats // 2
    for i in range(2):
        at = pl.ds(i * step, step)
        x = dot(table_ref[at, :], pick[...], 1, 0)
        squares += jnp.sum(x * x, axis=0, keepdims=True)
        scaled[at, :] = (gain_ref[at, :] * x).astype(BF16)
    scale = lax.rsqrt(squares / feats + NORM_EPS)
    half = in_a.shape[0]
    for i, w in enumerate((in_a, in_b)):
        pre = dot(w[...], scaled[...], 1, 0) * scale
        hidden[pl.ds(i * half, half), :] = jax.nn.gelu(pre, approximate=True).astype(BF16)
    total = dot(out_a[...], hidden[:half, :], 0, 0) + dot(out_b[...], hidden[half:, :], 0, 0)
    part_ref[...] = total.astype(BF16).reshape(part_ref.shape)


def finish_kernel(parts_ref, emb_ref, out_ref):
    total = emb_ref[...].astype(F32)
    for i in range(parts_ref.shape[0]):
        total += parts_ref[i].astype(F32)
    encoded = total.astype(BF16)
    cols = encoded.shape[1]
    sources = out_ref.shape[0]
    n = sources * SLOTS
    row, col = iota((n, cols), 0), iota((n, cols), 1)
    place = hot((row // SLOTS) * CAP + row % SLOTS == col)
    place = jnp.where(row % SLOTS < CAP, place, jnp.zeros_like(place))
    out_ref[...] = dot(place, encoded, 1, 1).astype(BF16).reshape(out_ref.shape)


def place_kernel(back_ref, slot_ref, out_ref):
    back = back_ref[...].reshape(-1, back_ref.shape[2])
    n, toks = back.shape[0], slot_ref.shape[1]
    pick = hot(iota((n, toks), 0) == slot_ref[...])
    out_ref[...] = dot(back, pick, 0, 0).astype(BF16)


def call(kernel, out_shape, scratch=(), vmem=32 * 1024 * 1024):
    return pl.pallas_call(
        kernel,
        out_shape=out_shape,
        scratch_shapes=list(scratch),
        compiler_params=pltpu.CompilerParams(vmem_limit_bytes=vmem),
    )


def on_device(neighbour_ids, table_cols, gain, w_in, w_out):
    seq = ("y", "z")
    owners = lax.axis_size(seq)
    chips = lax.axis_size("x")
    feat_local, rows = table_cols.shape
    feats, half = w_in.shape
    toks = neighbour_ids.shape[0]
    cols = owners * CAP
    shape = jax.ShapeDtypeStruct

    ids = neighbour_ids.reshape(1, toks)
    outgoing, slot = call(
        functools.partial(request_kernel, rows),
        (shape((owners, 1, SLOTS), I32), shape((1, toks), I32)),
    )(ids)
    table = lax.all_gather(table_cols, ("x", "core"), axis=0, tiled=True)
    block = lax.all_to_all(outgoing, seq, split_axis=0, concat_axis=0, tiled=True)

    core = lax.axis_index("core")
    swap = [(0, 1), (1, 0)]
    w_in_t = w_in.T
    by_core = w_out.reshape(half, chips, 2, feat_local)
    out_mine = lax.dynamic_index_in_dim(by_core, core, 2, False).reshape(half, chips * feat_local)
    out_send = lax.dynamic_index_in_dim(by_core, 1 - core, 2, False).reshape(half, chips * feat_local)
    in_other = lax.ppermute(w_in_t, "core", swap)
    out_other = lax.ppermute(out_send, "core", swap)

    parts, emb = call(
        layer_kernel,
        (shape((chips, feat_local, cols), BF16), shape((feat_local, cols), BF16)),
        (pltpu.VMEM((rows, cols), BF16), pltpu.VMEM((feats, cols), BF16), pltpu.VMEM((2 * half, cols), BF16)),
    )(block, table, table_cols, gain.reshape(feats, 1), w_in_t, in_other, out_mine, out_other)
    parts = lax.all_to_all(parts, "x", split_axis=0, concat_axis=0, tiled=True)
    encoded = call(finish_kernel, shape((owners, SLOTS, feat_local), BF16))(parts, emb)
    back = lax.all_to_all(encoded, seq, split_axis=0, concat_axis=0, tiled=True)
    return call(place_kernel, shape((feat_local, toks), BF16))(back, slot)


def solution(mesh):
    fine = Mesh(mesh.devices.reshape(8, 12, 4, 2), ("y", "z", "x", "core"))
    seq, vocab = ("y", "z"), ("x", "core")
    in_specs = (P(seq), P(vocab, seq), P(), P(None, vocab), P(vocab, None))
    return jax.shard_map(
        on_device, mesh=fine, in_specs=in_specs, out_specs=P(vocab, seq), check_vma=False
    )
```

```python
import functools

import jax
import jax.numpy as jnp
from jax import lax
from jax.experimental import pallas as pl
from jax.experimental.pallas import tpu as pltpu
from jax.sharding import Mesh, PartitionSpec as P

CAP = 6
SLOTS = 8
SPLIT = 64
NORM_EPS = 1e-05
F32 = jnp.float32
BF16 = jnp.bfloat16
I32 = jnp.int32


def iota(shape, dim):
    return lax.broadcasted_iota(I32, shape, dim)


def hot(mask):
    return jnp.where(mask, 1.0, 0.0).astype(BF16)


def dot(a, b, ca, cb):
    return lax.dot_general(a, b, (((ca,), (cb,)), ((), ())), preferred_element_type=F32)


def request_kernel(rows, ids_ref, out_ref, slot_ref):
    owners, toks = out_ref.shape[0], ids_ref.shape[1]
    ids = ids_ref[...]
    owner = ids // rows
    code = ids - owner * rows + 1
    mine = iota((owners, toks), 0) == owner
    mine_hot = hot(mine)
    earlier = hot(iota((toks, toks), 0) < iota((toks, toks), 1))
    count = dot(mine_hot, earlier, 1, 0)
    rank = jnp.sum(jnp.where(mine, count, 0.0), axis=0, keepdims=True).astype(I32)
    at = iota((SLOTS, toks), 0) == rank
    high = jnp.where(at, code // SPLIT, 0).astype(F32).astype(BF16)
    low = jnp.where(at, code % SPLIT, 0).astype(F32).astype(BF16)
    out = dot(mine_hot, high, 1, 1) * SPLIT + dot(mine_hot, low, 1, 1)
    out_ref[:, 0, :] = out.astype(I32)
    slot_ref[...] = owner * SLOTS + rank


def third(r, block, count):
    return sum((r >= k * block).astype(I32) for k in range(1, count))


def blocks_kernel(w_ref, mine_ref, send_ref):
    core = lax.axis_index("core")
    n, m = mine_ref.shape[0], w_ref.shape[1]
    row, lane = iota((n, m), 0), iota((n, m), 1)
    block = n // lax.axis_size("x")
    base = row + third(row, block, n // block) * block
    w = w_ref[...]
    mine_ref[...] = dot(hot(lane == base + core * block), w, 1, 1).astype(BF16)
    send_ref[...] = dot(hot(lane == base + (1 - core) * block), w, 1, 1).astype(BF16)


def order_kernel(*refs):
    out_ref = refs[-1]
    chips = out_ref.shape[0]
    me = lax.axis_index("x")
    for k, ref in enumerate(refs[:-1]):
        out_ref[lax.rem(me - k + chips, chips)] = ref[...]


def layer_kernel(block_ref, mine_ref, other_ref, gain_ref, in_a, in_b, out_a, out_b,
                 part_ref, emb_ref, pick, scaled, hidden, own):
    core, chip = lax.axis_index("core"), lax.axis_index("x")
    sources = block_ref.shape[0]
    chips, step, rows = mine_ref.shape
    feats = 2 * chips * step
    cols = sources * CAP
    code = block_ref[:, 0, :]
    spread = hot(iota((sources, cols), 1) // CAP == iota((sources, cols), 0))
    high = (code // SPLIT).astype(F32).astype(BF16)
    low = (code % SPLIT).astype(F32).astype(BF16)
    wide = dot(high, spread, 0, 0) * SPLIT + dot(low, spread, 0, 0)
    lane = iota((SLOTS, cols), 1)
    local = jnp.sum(jnp.where(lane - (lane // CAP) * CAP == iota((SLOTS, cols), 0), wide, 0.0), axis=0, keepdims=True)
    local = local.astype(I32) - 1
    pick[...] = hot(iota((rows, cols), 0) == local)
    squares = jnp.zeros((1, cols), F32)
    for ref, side in ((mine_ref, core), (other_ref, 1 - core)):
        x = dot(ref[...].reshape(chips * step, rows), pick[...], 1, 0)
        squares += jnp.sum(x * x, axis=0, keepdims=True)
        for i in range(chips):
            part = x[i * step:(i + 1) * step]
            at = pl.ds(pl.multiple_of((2 * i + side) * step, 16), step)
            scaled[at, :] = (gain_ref[at, :] * part).astype(BF16)
            if ref is mine_ref:
                own[i] = part.astype(BF16)
    emb_ref[...] = own[chip]
    scale = lax.rsqrt(squares / feats + NORM_EPS)
    half = in_a.shape[0]
    for i, w in enumerate((in_a, in_b)):
        pre = dot(w[...], scaled[...], 1, 0) * scale
        hidden[pl.ds(i * half, half), :] = jax.nn.gelu(pre, approximate=True).astype(BF16)
    total = dot(out_a[...], hidden[:half, :], 1, 0) + dot(out_b[...], hidden[half:, :], 1, 0)
    part_ref[...] = total.astype(BF16).reshape(part_ref.shape)


def finish_kernel(parts_ref, emb_ref, out_ref):
    total = emb_ref[...].astype(F32)
    for i in range(parts_ref.shape[0]):
        total += parts_ref[i].astype(F32)
    encoded = total.astype(BF16)
    cols = encoded.shape[1]
    sources = out_ref.shape[0]
    n = sources * SLOTS
    row, col = iota((n, cols), 0), iota((n, cols), 1)
    place = hot((row // SLOTS) * CAP + row % SLOTS == col)
    place = jnp.where(row % SLOTS < CAP, place, jnp.zeros_like(place))
    out_ref[...] = dot(place, encoded, 1, 1).astype(BF16).reshape(out_ref.shape)


def place_kernel(back_ref, slot_ref, out_ref):
    back = back_ref[...].reshape(-1, back_ref.shape[2])
    n, toks = back.shape[0], slot_ref.shape[1]
    pick = hot(iota((n, toks), 0) == slot_ref[...])
    out_ref[...] = dot(back, pick, 0, 0).astype(BF16)


def call(kernel, out_shape, scratch=(), vmem=32 * 1024 * 1024):
    return pl.pallas_call(
        kernel,
        out_shape=out_shape,
        scratch_shapes=list(scratch),
        compiler_params=pltpu.CompilerParams(vmem_limit_bytes=vmem),
    )


def on_device(neighbour_ids, table_cols, gain, w_in, w_out):
    seq = ("y", "z")
    owners = lax.axis_size(seq)
    chips = lax.axis_size("x")
    feat_local, rows = table_cols.shape
    feats, half = w_in.shape
    toks = neighbour_ids.shape[0]
    cols = owners * CAP
    shape = jax.ShapeDtypeStruct

    ids = neighbour_ids.reshape(1, toks)
    behind = [
        lax.ppermute(table_cols, "x", [(i, (i + k) % chips) for i in range(chips)])
        for k in range(1, chips)
    ]
    outgoing, slot = call(
        functools.partial(request_kernel, rows),
        (shape((owners, 1, SLOTS), I32), shape((1, toks), I32)),
    )(ids)
    block = lax.all_to_all(outgoing, seq, split_axis=0, concat_axis=0, tiled=True)

    swap = [(0, 1), (1, 0)]
    w_in_t = w_in.T
    w_out, _ = lax.optimization_barrier((w_out, slot))
    w_swap, _ = lax.optimization_barrier((w_in_t, slot))
    out_mine, out_send = call(blocks_kernel, (shape((chips * feat_local, half), BF16),) * 2)(w_out)
    in_other = lax.ppermute(w_swap, "core", swap)
    out_other = lax.ppermute(out_send, "core", swap)
    own_table, _ = lax.optimization_barrier((table_cols, slot))
    mine = call(order_kernel, shape((chips, feat_local, rows), BF16))(own_table, *behind)
    other = lax.ppermute(mine, "core", swap)

    parts, emb = call(
        layer_kernel,
        (shape((chips, feat_local, cols), BF16), shape((feat_local, cols), BF16)),
        (
            pltpu.VMEM((rows, cols), BF16),
            pltpu.VMEM((feats, cols), BF16),
            pltpu.VMEM((2 * half, cols), BF16),
            pltpu.VMEM((chips, feat_local, cols), BF16),
        ),
    )(block, mine, other, gain.reshape(feats, 1), w_in_t, in_other, out_mine, out_other)
    parts = lax.all_to_all(parts, "x", split_axis=0, concat_axis=0, tiled=True)
    encoded = call(finish_kernel, shape((owners, SLOTS, feat_local), BF16))(parts, emb)
    back = lax.all_to_all(encoded, seq, split_axis=0, concat_axis=0, tiled=True)
    return call(place_kernel, shape((feat_local, toks), BF16))(back, slot)


def solution(mesh):
    fine = Mesh(mesh.devices.reshape(8, 12, 4, 2), ("y", "z", "x", "core"))
    seq, vocab = ("y", "z"), ("x", "core")
    in_specs = (P(seq), P(vocab, seq), P(), P(None, vocab), P(vocab, None))
    return jax.shard_map(
        on_device, mesh=fine, in_specs=in_specs, out_specs=P(vocab, seq), check_vma=False
    )
```

```python
import functools

import jax
import jax.numpy as jnp
from jax import lax
from jax.experimental import pallas as pl
from jax.experimental.pallas import tpu as pltpu
from jax.sharding import Mesh, PartitionSpec as P

CAP = 6
SLOTS = 8
SPLIT = 64
NORM_EPS = 1e-05
F32 = jnp.float32
BF16 = jnp.bfloat16
I32 = jnp.int32


def iota(shape, dim):
    return lax.broadcasted_iota(I32, shape, dim)


def hot(mask):
    return jnp.where(mask, 1.0, 0.0).astype(BF16)


def dot(a, b, ca, cb):
    return lax.dot_general(a, b, (((ca,), (cb,)), ((), ())), preferred_element_type=F32)


def ranked(ids, owners, rows):
    toks = ids.shape[1]
    owner = ids // rows
    mine = iota((owners, toks), 0) == owner
    mine_hot = hot(mine)
    earlier = hot(iota((toks, toks), 0) < iota((toks, toks), 1))
    count = dot(mine_hot, earlier, 1, 0)
    rank = jnp.sum(jnp.where(mine, count, 0.0), axis=0, keepdims=True).astype(I32)
    return owner, ids - owner * rows + 1, rank, mine_hot


def request_kernel(rows, ids_ref, out_ref):
    owner, code, rank, mine_hot = ranked(ids_ref[...], out_ref.shape[0], rows)
    at = iota((SLOTS, ids_ref.shape[1]), 0) == rank
    high = jnp.where(at, code // SPLIT, 0).astype(F32).astype(BF16)
    low = jnp.where(at, code % SPLIT, 0).astype(F32).astype(BF16)
    out = dot(mine_hot, high, 1, 1) * SPLIT + dot(mine_hot, low, 1, 1)
    out_ref[:, 0, :] = out.astype(I32)


def third(r, block, count):
    return sum((r >= k * block).astype(I32) for k in range(1, count))


def blocks_kernel(owners, rows, w_ref, ids_ref, mine_ref, send_ref, slot_ref):
    owner, _, rank, _ = ranked(ids_ref[...], owners, rows)
    slot_ref[...] = owner * SLOTS + rank
    core = lax.axis_index("core")
    n, m = mine_ref.shape[0], w_ref.shape[1]
    row, lane = iota((n, m), 0), iota((n, m), 1)
    block = n // lax.axis_size("x")
    base = row + third(row, block, n // block) * block
    w = w_ref[...]
    mine_ref[...] = dot(hot(lane == base + core * block), w, 1, 1).astype(BF16)
    send_ref[...] = dot(hot(lane == base + (1 - core) * block), w, 1, 1).astype(BF16)


def order_kernel(*refs):
    out_ref = refs[-1]
    chips = out_ref.shape[0]
    me = lax.axis_index("x")
    for k, ref in enumerate(refs[:-1]):
        out_ref[lax.rem(me - k + chips, chips)] = ref[...]


def pick_kernel(block_ref, pick_ref):
    sources = block_ref.shape[0]
    rows, cols = pick_ref.shape
    code = block_ref[:, 0, :]
    spread = hot(iota((sources, cols), 1) // CAP == iota((sources, cols), 0))
    high = (code // SPLIT).astype(F32).astype(BF16)
    low = (code % SPLIT).astype(F32).astype(BF16)
    wide = dot(high, spread, 0, 0) * SPLIT + dot(low, spread, 0, 0)
    lane = iota((SLOTS, cols), 1)
    local = jnp.sum(jnp.where(lane - (lane // CAP) * CAP == iota((SLOTS, cols), 0), wide, 0.0), axis=0, keepdims=True)
    local = local.astype(I32) - 1
    pick_ref[...] = hot(iota((rows, cols), 0) == local)


def layer_kernel(pick, mine_ref, other_ref, gain_ref, in_a, in_b, out_a, out_b,
                 part_ref, emb_ref, scaled, hidden, own):
    core, chip = lax.axis_index("core"), lax.axis_index("x")
    chips, step, rows = mine_ref.shape
    feats = 2 * chips * step
    cols = pick.shape[1]
    squares = jnp.zeros((1, cols), F32)
    for ref, side in ((mine_ref, core), (other_ref, 1 - core)):
        x = dot(ref[...].reshape(chips * step, rows), pick[...], 1, 0)
        squares += jnp.sum(x * x, axis=0, keepdims=True)
        for i in range(chips):
            part = x[i * step:(i + 1) * step]
            at = pl.ds(pl.multiple_of((2 * i + side) * step, 16), step)
            scaled[at, :] = (gain_ref[at, :] * part).astype(BF16)
            if ref is mine_ref:
                own[i] = part.astype(BF16)
    emb_ref[...] = own[chip]
    scale = lax.rsqrt(squares / feats + NORM_EPS)
    half = in_a.shape[0]
    for i, w in enumerate((in_a, in_b)):
        pre = dot(w[...], scaled[...], 1, 0) * scale
        hidden[pl.ds(i * half, half), :] = jax.nn.gelu(pre, approximate=True).astype(BF16)
    total = dot(out_a[...], hidden[:half, :], 1, 0) + dot(out_b[...], hidden[half:, :], 1, 0)
    part_ref[...] = total.astype(BF16).reshape(part_ref.shape)


def finish_kernel(parts_ref, emb_ref, out_ref):
    total = emb_ref[...].astype(F32)
    for i in range(parts_ref.shape[0]):
        total += parts_ref[i].astype(F32)
    encoded = total.astype(BF16)
    cols = encoded.shape[1]
    sources = out_ref.shape[0]
    n = sources * SLOTS
    row, col = iota((n, cols), 0), iota((n, cols), 1)
    place = hot((row // SLOTS) * CAP + row % SLOTS == col)
    place = jnp.where(row % SLOTS < CAP, place, jnp.zeros_like(place))
    out_ref[...] = dot(place, encoded, 1, 1).astype(BF16).reshape(out_ref.shape)


def place_kernel(back_ref, slot_ref, out_ref):
    back = back_ref[...].reshape(-1, back_ref.shape[2])
    n, toks = back.shape[0], slot_ref.shape[1]
    pick = hot(iota((n, toks), 0) == slot_ref[...])
    out_ref[...] = dot(back, pick, 0, 0).astype(BF16)


def call(kernel, out_shape, scratch=(), vmem=32 * 1024 * 1024, flops=None):
    return pl.pallas_call(
        kernel,
        out_shape=out_shape,
        scratch_shapes=list(scratch),
        cost_estimate=flops and pl.CostEstimate(flops=flops, bytes_accessed=0, transcendentals=0),
        compiler_params=pltpu.CompilerParams(vmem_limit_bytes=vmem),
    )


def on_device(neighbour_ids, table_cols, gain, w_in, w_out):
    seq = ("y", "z")
    owners = lax.axis_size(seq)
    chips = lax.axis_size("x")
    feat_local, rows = table_cols.shape
    feats, half = w_in.shape
    toks = neighbour_ids.shape[0]
    cols = owners * CAP
    shape = jax.ShapeDtypeStruct

    ids = neighbour_ids.reshape(1, toks)
    behind = [
        lax.ppermute(table_cols, "x", [(i, (i + k) % chips) for i in range(chips)])
        for k in range(1, chips)
    ]
    outgoing = call(functools.partial(request_kernel, rows), shape((owners, 1, SLOTS), I32))(ids)
    block = lax.all_to_all(outgoing, seq, split_axis=0, concat_axis=0, tiled=True)

    swap = [(0, 1), (1, 0)]
    w_in_t = w_in.T
    out_mine, out_send, slot = call(
        functools.partial(blocks_kernel, owners, rows),
        (shape((chips * feat_local, half), BF16),) * 2 + (shape((1, toks), I32),),
    )(w_out, ids)
    in_other = lax.ppermute(w_in_t, "core", swap)
    out_other = lax.ppermute(out_send, "core", swap)
    mine = call(order_kernel, shape((chips, feat_local, rows), BF16))(table_cols, *behind)
    other = lax.ppermute(mine, "core", swap)

    pick = call(pick_kernel, shape((rows, cols), BF16), flops=30_000_000_000)(block)
    parts, emb = call(
        layer_kernel,
        (shape((chips, feat_local, cols), BF16), shape((feat_local, cols), BF16)),
        (
            pltpu.VMEM((feats, cols), BF16),
            pltpu.VMEM((2 * half, cols), BF16),
            pltpu.VMEM((chips, feat_local, cols), BF16),
        ),
    )(pick, mine, other, gain.reshape(feats, 1), w_in_t, in_other, out_mine, out_other)
    parts = lax.all_to_all(parts, "x", split_axis=0, concat_axis=0, tiled=True)
    encoded = call(finish_kernel, shape((owners, SLOTS, feat_local), BF16))(parts, emb)
    back = lax.all_to_all(encoded, seq, split_axis=0, concat_axis=0, tiled=True)
    return call(place_kernel, shape((feat_local, toks), BF16))(back, slot)


def solution(mesh):
    fine = Mesh(mesh.devices.reshape(8, 12, 4, 2), ("y", "z", "x", "core"))
    seq, vocab = ("y", "z"), ("x", "core")
    in_specs = (P(seq), P(vocab, seq), P(), P(None, vocab), P(vocab, None))
    return jax.shard_map(
        on_device, mesh=fine, in_specs=in_specs, out_specs=P(vocab, seq), check_vma=False
    )
```

```python
import functools

import jax
import jax.numpy as jnp
from jax import lax
from jax.experimental import pallas as pl
from jax.experimental.pallas import tpu as pltpu
from jax.sharding import Mesh, PartitionSpec as P

CAP = 6
SLOTS = 8
SPLIT = 64
NORM_EPS = 1e-05
F32 = jnp.float32
BF16 = jnp.bfloat16
I32 = jnp.int32


def iota(shape, dim):
    return lax.broadcasted_iota(I32, shape, dim)


def hot(mask):
    return jnp.where(mask, 1.0, 0.0).astype(BF16)


def dot(a, b, ca, cb):
    return lax.dot_general(a, b, (((ca,), (cb,)), ((), ())), preferred_element_type=F32)


def ranked(ids, owners, rows):
    toks = ids.shape[1]
    owner = ids // rows
    mine = iota((owners, toks), 0) == owner
    mine_hot = hot(mine)
    earlier = hot(iota((toks, toks), 0) < iota((toks, toks), 1))
    count = dot(mine_hot, earlier, 1, 0)
    rank = jnp.sum(jnp.where(mine, count, 0.0), axis=0, keepdims=True).astype(I32)
    return owner, ids - owner * rows + 1, rank, mine_hot


def request_kernel(rows, ids_ref, out_ref):
    owner, code, rank, mine_hot = ranked(ids_ref[...], out_ref.shape[0], rows)
    at = iota((SLOTS, ids_ref.shape[1]), 0) == rank
    high = jnp.where(at, code // SPLIT, 0).astype(F32).astype(BF16)
    low = jnp.where(at, code % SPLIT, 0).astype(F32).astype(BF16)
    out = dot(mine_hot, high, 1, 1) * SPLIT + dot(mine_hot, low, 1, 1)
    out_ref[:, 0, :] = out.astype(I32)


def third(r, block, count):
    return sum((r >= k * block).astype(I32) for k in range(1, count))


def blocks_kernel(owners, rows, chips, in_ref, out_ref, gain_ref, ids_ref, mine_ref, send_ref, gains_ref, slot_ref):
    owner, _, rank, _ = ranked(ids_ref[...], owners, rows)
    slot_ref[...] = owner * SLOTS + rank
    core = lax.axis_index("core")
    half, feats = in_ref.shape
    n = feats // 2
    block = n // chips
    gain = gain_ref[...]
    w_in, w_out = in_ref[...], out_ref[...]
    row, lane = iota((n, feats), 0), iota((n, feats), 1)
    base = row + third(row, block, chips) * block
    for i, side in enumerate((core, 1 - core)):
        mask = lane == base + side * block
        gains_ref[i] = jnp.sum(jnp.where(mask, gain, 0.0), axis=1, keepdims=True)
        pick = hot(mask)
        part = dot(w_in, pick, 1, 1).astype(BF16)
        mine_ref[i] = part
        send_ref[1 - i] = part
        rest = dot(pick, w_out, 1, 1).astype(BF16)
        if i:
            send_ref[2] = rest
        else:
            mine_ref[2] = rest


def pick_kernel(block_ref, pick_ref):
    sources = block_ref.shape[0]
    rows, cols = pick_ref.shape
    code = block_ref[:, 0, :]
    spread = hot(iota((sources, cols), 1) // CAP == iota((sources, cols), 0))
    high = (code // SPLIT).astype(F32).astype(BF16)
    low = (code % SPLIT).astype(F32).astype(BF16)
    wide = dot(high, spread, 0, 0) * SPLIT + dot(low, spread, 0, 0)
    lane = iota((SLOTS, cols), 1)
    local = jnp.sum(jnp.where(lane - (lane // CAP) * CAP == iota((SLOTS, cols), 0), wide, 0.0), axis=0, keepdims=True)
    local = local.astype(I32) - 1
    pick_ref[...] = hot(iota((rows, cols), 0) == local)


def select_kernel(pick_ref, *refs):
    out_ref, table = refs[-2:]
    chips, step = out_ref.shape[0], out_ref.shape[1]
    me = lax.axis_index("x")
    for k, ref in enumerate(refs[:-2]):
        table[lax.rem(me - k + chips, chips)] = ref[...]
    x = dot(table[...].reshape(chips * step, -1), pick_ref[...], 1, 0)
    out_ref[...] = x.astype(BF16).reshape(out_ref.shape)


def scaled_of(x_ref, gain):
    chips, step, cols = x_ref.shape
    x = x_ref[...].reshape(chips * step, cols).astype(F32)
    return (gain * x).astype(BF16), jnp.sum(x * x, axis=0, keepdims=True)


def first_kernel(x_ref, gains_ref, mine_ref, other_ref, pre_ref, square_ref):
    scaled, square_ref[...] = scaled_of(x_ref, gains_ref[0])
    for i, w in enumerate((mine_ref, other_ref)):
        pre_ref[i] = dot(w[0], scaled, 1, 0)


def second_kernel(x_ref, gains_ref, mine_ref, other_ref, pre_ref, square_ref, out_ref, hidden):
    scaled, squares = scaled_of(x_ref, gains_ref[1])
    squares += square_ref[...]
    scale = lax.rsqrt(squares / (2 * scaled.shape[0]) + NORM_EPS)
    for i, w in enumerate((mine_ref, other_ref)):
        pre = (pre_ref[i] + dot(w[1], scaled, 1, 0)) * scale
        hidden[i] = jax.nn.gelu(pre, approximate=True).astype(BF16)
    total = dot(mine_ref[2], hidden[0], 1, 0) + dot(other_ref[2], hidden[1], 1, 0)
    out_ref[...] = total.astype(BF16).reshape(out_ref.shape)


def finish_kernel(parts_ref, x_ref, out_ref):
    total = x_ref[lax.axis_index("x")].astype(F32)
    for i in range(parts_ref.shape[0]):
        total += parts_ref[i].astype(F32)
    encoded = total.astype(BF16)
    cols = encoded.shape[1]
    sources = out_ref.shape[0]
    n = sources * SLOTS
    row, col = iota((n, cols), 0), iota((n, cols), 1)
    place = hot((row // SLOTS) * CAP + row % SLOTS == col)
    place = jnp.where(row % SLOTS < CAP, place, jnp.zeros_like(place))
    out_ref[...] = dot(place, encoded, 1, 1).astype(BF16).reshape(out_ref.shape)


def place_kernel(back_ref, slot_ref, out_ref):
    back = back_ref[...].reshape(-1, back_ref.shape[2])
    n, toks = back.shape[0], slot_ref.shape[1]
    pick = hot(iota((n, toks), 0) == slot_ref[...])
    out_ref[...] = dot(back, pick, 0, 0).astype(BF16)


def call(kernel, out_shape, scratch=(), vmem=32 * 1024 * 1024, flops=None):
    return pl.pallas_call(
        kernel,
        out_shape=out_shape,
        scratch_shapes=list(scratch),
        cost_estimate=flops and pl.CostEstimate(flops=flops, bytes_accessed=0, transcendentals=0),
        compiler_params=pltpu.CompilerParams(vmem_limit_bytes=vmem),
    )


def on_device(neighbour_ids, table_cols, gain, w_in, w_out):
    seq = ("y", "z")
    owners = lax.axis_size(seq)
    chips = lax.axis_size("x")
    feat_local, rows = table_cols.shape
    feats, half = w_in.shape
    toks = neighbour_ids.shape[0]
    cols = owners * CAP
    shape = jax.ShapeDtypeStruct

    ids = neighbour_ids.reshape(1, toks)
    outgoing = call(functools.partial(request_kernel, rows), shape((owners, 1, SLOTS), I32))(ids)
    block = lax.all_to_all(outgoing, seq, split_axis=0, concat_axis=0, tiled=True)
    behind = [
        lax.ppermute(table_cols, "x", [(i, (i + k) % chips) for i in range(chips)])
        for k in range(1, chips)
    ]
    swap = [(0, 1), (1, 0)]
    w_mine, w_send, gains, slot = call(
        functools.partial(blocks_kernel, owners, rows, chips),
        (shape((3, half, half), BF16),) * 2 + (shape((2, half, 1), F32), shape((1, toks), I32)),
    )(w_in.T, w_out, gain.reshape(1, feats), ids)
    w_other = lax.ppermute(w_send, "core", swap)

    pick = call(pick_kernel, shape((rows, cols), BF16), flops=10_000_000_000)(block)
    x_mine = call(
        select_kernel,
        shape((chips, feat_local, cols), BF16),
        (pltpu.VMEM((chips, feat_local, rows), BF16),),
    )(pick, table_cols, *behind)
    x_other = lax.ppermute(x_mine, "core", swap)
    pre, square = call(first_kernel, (shape((2, half, cols), F32), shape((1, cols), F32)))(
        x_mine, gains, w_mine, w_other
    )
    parts = call(second_kernel, shape((chips, feat_local, cols), BF16), (pltpu.VMEM((2, half, cols), BF16),))(
        x_other, gains, w_mine, w_other, pre, square
    )
    parts = lax.all_to_all(parts, "x", split_axis=0, concat_axis=0, tiled=True)
    encoded = call(finish_kernel, shape((owners, SLOTS, feat_local), BF16))(parts, x_mine)
    back = lax.all_to_all(encoded, seq, split_axis=0, concat_axis=0, tiled=True)
    return call(place_kernel, shape((feat_local, toks), BF16))(back, slot)


def solution(mesh):
    fine = Mesh(mesh.devices.reshape(8, 12, 4, 2), ("y", "z", "x", "core"))
    seq, vocab = ("y", "z"), ("x", "core")
    in_specs = (P(seq), P(vocab, seq), P(), P(None, vocab), P(vocab, None))
    return jax.shard_map(
        on_device, mesh=fine, in_specs=in_specs, out_specs=P(vocab, seq), check_vma=False
    )
```

```python
import functools

import jax
import jax.numpy as jnp
from jax import lax
from jax.experimental import pallas as pl
from jax.experimental.pallas import tpu as pltpu
from jax.sharding import Mesh, PartitionSpec as P

CAP = 6
SLOTS = 8
SPLIT = 64
NORM_EPS = 1e-05
F32 = jnp.float32
BF16 = jnp.bfloat16
I32 = jnp.int32


def iota(shape, dim):
    return lax.broadcasted_iota(I32, shape, dim)


def hot(mask):
    return jnp.where(mask, 1.0, 0.0).astype(BF16)


def dot(a, b, ca, cb):
    return lax.dot_general(a, b, (((ca,), (cb,)), ((), ())), preferred_element_type=F32)


def ranked(ids, owners, rows):
    toks = ids.shape[1]
    owner = ids // rows
    mine = iota((owners, toks), 0) == owner
    mine_hot = hot(mine)
    earlier = hot(iota((toks, toks), 0) < iota((toks, toks), 1))
    count = dot(mine_hot, earlier, 1, 0)
    rank = jnp.sum(jnp.where(mine, count, 0.0), axis=0, keepdims=True).astype(I32)
    return owner, ids - owner * rows + 1, rank, mine_hot


def request_kernel(rows, ids_ref, out_ref):
    owner, code, rank, mine_hot = ranked(ids_ref[...], out_ref.shape[0], rows)
    at = iota((SLOTS, ids_ref.shape[1]), 0) == rank
    high = jnp.where(at, code // SPLIT, 0).astype(F32).astype(BF16)
    low = jnp.where(at, code % SPLIT, 0).astype(F32).astype(BF16)
    out = dot(mine_hot, high, 1, 1) * SPLIT + dot(mine_hot, low, 1, 1)
    out_ref[:, 0, :] = out.astype(I32)


def third(r, block, count):
    return sum((r >= k * block).astype(I32) for k in range(1, count))


def blocks_kernel(owners, rows, chips, in_hbm, out_hbm, gain_ref, ids_ref, mine_ref, send_ref, gains_ref, slot_ref,
                  w_in, w_out, sems):
    load_in = pltpu.make_async_copy(in_hbm, w_in, sems.at[0])
    load_out = pltpu.make_async_copy(out_hbm, w_out, sems.at[1])
    load_in.start()
    load_out.start()
    owner, _, rank, _ = ranked(ids_ref[...], owners, rows)
    slot_ref[...] = owner * SLOTS + rank
    core = lax.axis_index("core")
    half, feats = w_in.shape
    n = feats // 2
    block = n // chips
    gain = jnp.transpose(jnp.broadcast_to(gain_ref[...].reshape(1, feats), (8, feats)))[:, :1]
    for i in range(chips):
        for j in range(2):
            at = (2 * i + j) * block
            gains_ref[jnp.where(core == j, 0, 1), pl.ds(i * block, block), :] = gain[at:at + block]
    row, lane = iota((n, feats), 0), iota((n, feats), 1)
    base = row + third(row, block, chips) * block
    picks = [hot(lane == base + side * block) for side in (core, 1 - core)]
    load_in.wait()
    for i, pick in enumerate(picks):
        part = dot(w_in[...], pick, 1, 1).astype(BF16)
        mine_ref[i] = part
        send_ref[1 - i] = part
    load_out.wait()
    mine_ref[2] = dot(picks[0], w_out[...], 1, 1).astype(BF16)
    send_ref[2] = dot(picks[1], w_out[...], 1, 1).astype(BF16)


def decode_kernel(block_ref, out_ref):
    sources, cols = block_ref.shape[0], out_ref.shape[1]
    code = block_ref[:, 0, :]
    spread = hot(iota((sources, cols), 1) // CAP == iota((sources, cols), 0))
    high = (code // SPLIT).astype(F32).astype(BF16)
    low = (code % SPLIT).astype(F32).astype(BF16)
    wide = dot(high, spread, 0, 0) * SPLIT + dot(low, spread, 0, 0)
    lane = iota((SLOTS, cols), 1)
    local = jnp.sum(jnp.where(lane - (lane // CAP) * CAP == iota((SLOTS, cols), 0), wide, 0.0), axis=0, keepdims=True)
    out_ref[...] = local.astype(I32) - 1


def select_kernel(local_ref, *refs):
    blocks, (out_ref, table, sems) = refs[:-3], refs[-3:]
    chips, step, cols = out_ref.shape
    rows = table.shape[2]
    me = lax.axis_index("x")
    loads = [
        pltpu.make_async_copy(ref, table.at[lax.rem(me - k + chips, chips)], sems.at[k])
        for k, ref in enumerate(blocks)
    ]
    for load in loads:
        load.start()
    pick = hot(iota((rows, cols), 0) == local_ref[...])
    for load in loads:
        load.wait()
    x = dot(table[...].reshape(chips * step, rows), pick, 1, 0)
    out_ref[...] = x.astype(BF16).reshape(out_ref.shape)


def scaled_of(x_ref, gain):
    chips, step, cols = x_ref.shape
    x = x_ref[...].reshape(chips * step, cols).astype(F32)
    return (gain * x).astype(BF16), jnp.sum(x * x, axis=0, keepdims=True)


def first_kernel(x_ref, gains_ref, mine_ref, other_ref, pre_ref, square_ref):
    scaled, square_ref[...] = scaled_of(x_ref, gains_ref[0])
    for i, w in enumerate((mine_ref, other_ref)):
        pre_ref[i] = dot(w[0], scaled, 1, 0)


def second_kernel(x_ref, gains_ref, mine_ref, other_ref, pre_ref, square_ref, out_ref, hidden):
    scaled, squares = scaled_of(x_ref, gains_ref[1])
    squares += square_ref[...]
    scale = lax.rsqrt(squares / (2 * scaled.shape[0]) + NORM_EPS)
    for i, w in enumerate((mine_ref, other_ref)):
        pre = (pre_ref[i] + dot(w[1], scaled, 1, 0)) * scale
        hidden[i] = jax.nn.gelu(pre, approximate=True).astype(BF16)
    total = dot(mine_ref[2], hidden[0], 1, 0) + dot(other_ref[2], hidden[1], 1, 0)
    out_ref[...] = total.astype(BF16).reshape(out_ref.shape)


def finish_kernel(parts_ref, x_ref, out_ref):
    total = x_ref[lax.axis_index("x")].astype(F32)
    for i in range(parts_ref.shape[0]):
        total += parts_ref[i].astype(F32)
    encoded = total.astype(BF16)
    cols = encoded.shape[1]
    sources = out_ref.shape[0]
    n = sources * SLOTS
    row, col = iota((n, cols), 0), iota((n, cols), 1)
    place = hot((row // SLOTS) * CAP + row % SLOTS == col)
    place = jnp.where(row % SLOTS < CAP, place, jnp.zeros_like(place))
    out_ref[...] = dot(place, encoded, 1, 1).astype(BF16).reshape(out_ref.shape)


def place_kernel(back_ref, slot_ref, out_ref):
    back = back_ref[...].reshape(-1, back_ref.shape[2])
    n, toks = back.shape[0], slot_ref.shape[1]
    pick = hot(iota((n, toks), 0) == slot_ref[...])
    out_ref[...] = dot(back, pick, 0, 0).astype(BF16)


def call(kernel, out_shape, scratch=(), vmem=32 * 1024 * 1024, flops=None, **more):
    return pl.pallas_call(
        kernel,
        out_shape=out_shape,
        scratch_shapes=list(scratch),
        cost_estimate=flops and pl.CostEstimate(flops=flops, bytes_accessed=0, transcendentals=0),
        compiler_params=pltpu.CompilerParams(vmem_limit_bytes=vmem),
        **more,
    )


def on_device(neighbour_ids, table_cols, gain, w_in, w_out):
    seq = ("y", "z")
    owners = lax.axis_size(seq)
    chips = lax.axis_size("x")
    feat_local, rows = table_cols.shape
    feats, half = w_in.shape
    toks = neighbour_ids.shape[0]
    cols = owners * CAP
    shape = jax.ShapeDtypeStruct

    ids = neighbour_ids.reshape(1, toks)
    outgoing = call(functools.partial(request_kernel, rows), shape((owners, 1, SLOTS), I32))(ids)
    block = lax.all_to_all(outgoing, seq, split_axis=0, concat_axis=0, tiled=True)
    late_cols, _ = lax.optimization_barrier((table_cols, outgoing))

    def shifted(cols, k):
        return lax.ppermute(cols, "x", [(i, (i + k) % chips) for i in range(chips)])

    far = shifted(table_cols, 2)
    block, far = lax.optimization_barrier((block, far))
    behind = shifted(late_cols, 1), far, shifted(late_cols, 3)
    swap = [(0, 1), (1, 0)]
    anywhere, vmem = pl.BlockSpec(memory_space=pl.ANY), pl.BlockSpec(memory_space=pltpu.VMEM)
    w_mine, w_send, gains, slot = call(
        functools.partial(blocks_kernel, owners, rows, chips),
        (shape((3, half, half), BF16),) * 2 + (shape((2, half, 1), F32), shape((1, toks), I32)),
        (pltpu.VMEM((half, feats), BF16), pltpu.VMEM((half, feats), BF16), pltpu.SemaphoreType.DMA((2,))),
        in_specs=[anywhere, anywhere, vmem, vmem],
        vmem=60_000_000,
    )(w_in.T, w_out, gain, ids)
    w_other = lax.ppermute(w_send, "core", swap)

    local = call(decode_kernel, shape((1, cols), I32), flops=10_000_000_000)(block)
    x_mine = call(
        select_kernel,
        shape((chips, feat_local, cols), BF16),
        (pltpu.VMEM((chips, feat_local, rows), BF16), pltpu.SemaphoreType.DMA((chips,))),
        in_specs=[vmem] + [anywhere] * chips,
    )(local, table_cols, *behind)
    x_other = lax.ppermute(x_mine, "core", swap)
    pre, square = call(first_kernel, (shape((2, half, cols), F32), shape((1, cols), F32)))(
        x_mine, gains, w_mine, w_other
    )
    parts = call(second_kernel, shape((chips, feat_local, cols), BF16), (pltpu.VMEM((2, half, cols), BF16),))(
        x_other, gains, w_mine, w_other, pre, square
    )
    parts = lax.all_to_all(parts, "x", split_axis=0, concat_axis=0, tiled=True)
    encoded = call(finish_kernel, shape((owners, SLOTS, feat_local), BF16))(parts, x_mine)
    back = lax.all_to_all(encoded, seq, split_axis=0, concat_axis=0, tiled=True)
    return call(place_kernel, shape((feat_local, toks), BF16))(back, slot)


def solution(mesh):
    fine = Mesh(mesh.devices.reshape(8, 12, 4, 2), ("y", "z", "x", "core"))
    seq, vocab = ("y", "z"), ("x", "core")
    in_specs = (P(seq), P(vocab, seq), P(), P(None, vocab), P(vocab, None))
    return jax.shard_map(
        on_device, mesh=fine, in_specs=in_specs, out_specs=P(vocab, seq), check_vma=False
    )
```

```python
import functools

import jax
import jax.numpy as jnp
from jax import lax
from jax.experimental import pallas as pl
from jax.experimental.pallas import tpu as pltpu
from jax.sharding import Mesh, PartitionSpec as P

CAP = 6
SLOTS = 8
SPLIT = 64
NORM_EPS = 1e-05
F32 = jnp.float32
BF16 = jnp.bfloat16
I32 = jnp.int32


def iota(shape, dim):
    return lax.broadcasted_iota(I32, shape, dim)


def hot(mask):
    return jnp.where(mask, 1.0, 0.0).astype(BF16)


def dot(a, b, ca, cb):
    return lax.dot_general(a, b, (((ca,), (cb,)), ((), ())), preferred_element_type=F32)


def ranked(ids, owners, rows):
    toks = ids.shape[1]
    owner = ids // rows
    mine = iota((owners, toks), 0) == owner
    mine_hot = hot(mine)
    earlier = hot(iota((toks, toks), 0) < iota((toks, toks), 1))
    count = dot(mine_hot, earlier, 1, 0)
    rank = jnp.sum(jnp.where(mine, count, 0.0), axis=0, keepdims=True).astype(I32)
    return owner, ids - owner * rows + 1, rank, mine_hot


def request_kernel(rows, ids_ref, out_ref):
    owner, code, rank, mine_hot = ranked(ids_ref[...], out_ref.shape[0], rows)
    at = iota((SLOTS, ids_ref.shape[1]), 0) == rank
    high = jnp.where(at, code // SPLIT, 0).astype(F32).astype(BF16)
    low = jnp.where(at, code % SPLIT, 0).astype(F32).astype(BF16)
    out = dot(mine_hot, high, 1, 1) * SPLIT + dot(mine_hot, low, 1, 1)
    out_ref[:, 0, :] = out.astype(I32)


def third(r, block, count):
    return sum((r >= k * block).astype(I32) for k in range(1, count))


def blocks_kernel(owners, rows, chips, in_hbm, out_hbm, gain_ref, ids_ref, mine_ref, send_ref, gains_ref, slot_ref,
                  w_in, w_out, sems):
    load_in = pltpu.make_async_copy(in_hbm, w_in, sems.at[0])
    load_out = pltpu.make_async_copy(out_hbm, w_out, sems.at[1])
    load_in.start()
    load_out.start()
    owner, _, rank, _ = ranked(ids_ref[...], owners, rows)
    slot_ref[...] = owner * SLOTS + rank
    core = lax.axis_index("core")
    half, feats = w_in.shape
    n = feats // 2
    block = n // chips
    gain = jnp.transpose(jnp.broadcast_to(gain_ref[...].reshape(1, feats), (8, feats)))[:, :1]
    for i in range(chips):
        for j in range(2):
            at = (2 * i + j) * block
            gains_ref[jnp.where(core == j, 0, 1), pl.ds(i * block, block), :] = gain[at:at + block]
    row, lane = iota((n, feats), 0), iota((n, feats), 1)
    base = row + third(row, block, chips) * block
    picks = [hot(lane == base + side * block) for side in (core, 1 - core)]
    load_in.wait()
    for i, pick in enumerate(picks):
        part = dot(w_in[...], pick, 1, 1).astype(BF16)
        mine_ref[i] = part
        send_ref[1 - i] = part
    load_out.wait()
    mine_ref[2] = dot(picks[0], w_out[...], 1, 1).astype(BF16)
    send_ref[2] = dot(picks[1], w_out[...], 1, 1).astype(BF16)


def rows_kernel(block_ref, table_ref, out_ref):
    sources, rows = block_ref.shape[0], table_ref.shape[1]
    n = sources * SLOTS
    code = block_ref[:, 0, :]
    spread = hot(iota((n, sources), 0) // SLOTS == iota((n, sources), 1))
    high = (code // SPLIT).astype(F32).astype(BF16)
    low = (code % SPLIT).astype(F32).astype(BF16)
    wide = dot(spread, high, 1, 0) * SPLIT + dot(spread, low, 1, 0)
    row = iota((n, SLOTS), 0)
    local = jnp.sum(jnp.where(row % SLOTS == iota((n, SLOTS), 1), wide, 0.0), axis=1, keepdims=True)
    pick = hot(iota((n, rows), 1) == local.astype(I32) - 1)
    out_ref[...] = dot(pick, table_ref[...], 1, 1).astype(BF16).reshape(out_ref.shape)


def scaled_of(x_ref, gain):
    chips, step, cols = x_ref.shape
    x = x_ref[...].reshape(chips * step, cols).astype(F32)
    return (gain * x).astype(BF16), jnp.sum(x * x, axis=0, keepdims=True)


def first_kernel(x_ref, gains_ref, mine_ref, other_ref, pre_ref, square_ref):
    scaled, square_ref[...] = scaled_of(x_ref, gains_ref[0])
    for i, w in enumerate((mine_ref, other_ref)):
        pre_ref[i] = dot(w[0], scaled, 1, 0)


def second_kernel(x_ref, gains_ref, mine_ref, other_ref, pre_ref, square_ref, out_ref, hidden):
    scaled, squares = scaled_of(x_ref, gains_ref[1])
    squares += square_ref[...]
    scale = lax.rsqrt(squares / (2 * scaled.shape[0]) + NORM_EPS)
    for i, w in enumerate((mine_ref, other_ref)):
        pre = (pre_ref[i] + dot(w[1], scaled, 1, 0)) * scale
        hidden[i] = jax.nn.gelu(pre, approximate=True).astype(BF16)
    total = dot(mine_ref[2], hidden[0], 1, 0) + dot(other_ref[2], hidden[1], 1, 0)
    out_ref[...] = total.astype(BF16).reshape(out_ref.shape)


def place_kernel(back_ref, slot_ref, x_ref):
    back = back_ref[...].reshape(-1, back_ref.shape[2])
    n, toks = back.shape[0], slot_ref.shape[1]
    pick = hot(iota((n, toks), 0) == slot_ref[...])
    x = dot(back, pick, 0, 0).astype(BF16)
    for i in range(x_ref.shape[0]):
        x_ref[i] = x


def finish_kernel(parts_ref, x_ref, out_ref):
    total = x_ref[lax.axis_index("x")].astype(F32)
    for i in range(parts_ref.shape[0]):
        total += parts_ref[i].astype(F32)
    out_ref[...] = total.astype(BF16)


def call(kernel, out_shape, scratch=(), vmem=32 * 1024 * 1024, flops=None, **more):
    return pl.pallas_call(
        kernel,
        out_shape=out_shape,
        scratch_shapes=list(scratch),
        cost_estimate=flops and pl.CostEstimate(flops=flops, bytes_accessed=0, transcendentals=0),
        compiler_params=pltpu.CompilerParams(vmem_limit_bytes=vmem),
        **more,
    )


def on_device(neighbour_ids, table_cols, gain, w_in, w_out):
    seq = ("y", "z")
    owners = lax.axis_size(seq)
    chips = lax.axis_size("x")
    feat_local, rows = table_cols.shape
    feats, half = w_in.shape
    toks = neighbour_ids.shape[0]
    shape = jax.ShapeDtypeStruct

    ids = neighbour_ids.reshape(1, toks)
    outgoing = call(functools.partial(request_kernel, rows), shape((owners, 1, SLOTS), I32))(ids)
    block = lax.all_to_all(outgoing, seq, split_axis=0, concat_axis=0, tiled=True)
    swap = [(0, 1), (1, 0)]
    anywhere, vmem = pl.BlockSpec(memory_space=pl.ANY), pl.BlockSpec(memory_space=pltpu.VMEM)
    w_mine, w_send, gains, slot = call(
        functools.partial(blocks_kernel, owners, rows, chips),
        (shape((3, half, half), BF16),) * 2 + (shape((2, half, 1), F32), shape((1, toks), I32)),
        (pltpu.VMEM((half, feats), BF16), pltpu.VMEM((half, feats), BF16), pltpu.SemaphoreType.DMA((2,))),
        in_specs=[anywhere, anywhere, vmem, vmem],
        vmem=60_000_000,
    )(w_in.T, w_out, gain, ids)
    w_other = lax.ppermute(w_send, "core", swap)

    asked = call(rows_kernel, shape((owners, SLOTS, feat_local), BF16), flops=10_000_000_000)(block, table_cols)
    back = lax.all_to_all(asked, seq, split_axis=0, concat_axis=0, tiled=True)
    spread = call(place_kernel, shape((chips, feat_local, toks), BF16))(back, slot)
    x_mine = lax.all_to_all(spread, "x", split_axis=0, concat_axis=0, tiled=True)
    x_other = lax.ppermute(x_mine, "core", swap)
    pre, square = call(first_kernel, (shape((2, half, toks), F32), shape((1, toks), F32)))(
        x_mine, gains, w_mine, w_other
    )
    parts = call(second_kernel, shape((chips, feat_local, toks), BF16), (pltpu.VMEM((2, half, toks), BF16),))(
        x_other, gains, w_mine, w_other, pre, square
    )
    parts = lax.all_to_all(parts, "x", split_axis=0, concat_axis=0, tiled=True)
    return call(finish_kernel, shape((feat_local, toks), BF16))(parts, x_mine)


def solution(mesh):
    fine = Mesh(mesh.devices.reshape(8, 12, 4, 2), ("y", "z", "x", "core"))
    seq, vocab = ("y", "z"), ("x", "core")
    in_specs = (P(seq), P(vocab, seq), P(), P(None, vocab), P(vocab, None))
    return jax.shard_map(
        on_device, mesh=fine, in_specs=in_specs, out_specs=P(vocab, seq), check_vma=False
    )
```

```python
import functools

import jax
import jax.numpy as jnp
from jax import lax
from jax.experimental import pallas as pl
from jax.experimental.pallas import tpu as pltpu
from jax.sharding import Mesh, PartitionSpec as P

TALL, WIDE, LANES = 2, 3, 128
SLOTS = 8
SPLIT = 64
NORM_EPS = 1e-05
F32 = jnp.float32
BF16 = jnp.bfloat16
I32 = jnp.int32


def iota(shape, dim):
    return lax.broadcasted_iota(I32, shape, dim)


def hot(mask):
    return jnp.where(mask, 1.0, 0.0).astype(BF16)


def dot(a, b, ca, cb):
    return lax.dot_general(a, b, (((ca,), (cb,)), ((), ())), preferred_element_type=F32)


def ranked(ids, owners, rows):
    toks = ids.shape[1]
    owner = ids // rows
    mine = iota((owners, toks), 0) == owner
    mine_hot = hot(mine)
    earlier = hot(iota((toks, toks), 0) < iota((toks, toks), 1))
    count = dot(mine_hot, earlier, 1, 0)
    rank = jnp.sum(jnp.where(mine, count, 0.0), axis=0, keepdims=True).astype(I32)
    return owner, ids - owner * rows + 1, rank, mine_hot


def request_kernel(rows, ids_ref, out_ref):
    owner, code, rank, mine_hot = ranked(ids_ref[...], out_ref.shape[0], rows)
    at = iota((SLOTS, ids_ref.shape[1]), 0) == rank
    high = jnp.where(at, code // SPLIT, 0).astype(F32).astype(BF16)
    low = jnp.where(at, code % SPLIT, 0).astype(F32).astype(BF16)
    out = dot(mine_hot, high, 1, 1) * SPLIT + dot(mine_hot, low, 1, 1)
    out_ref[:, 0, :] = out.astype(I32)


def third(r, block, count):
    return sum((r >= k * block).astype(I32) for k in range(1, count))


def side_of(side, chips, n):
    row, lane = iota((n, 2 * n), 0), iota((n, 2 * n), 1)
    return hot(lane == row + third(row, n // chips, chips) * (n // chips) + side * (n // chips))


def send_kernel(chips, in_hbm, out_hbm, send_ref, mark_ref, w_in, w_out, sems):
    load_in = pltpu.make_async_copy(in_hbm, w_in, sems.at[0])
    load_out = pltpu.make_async_copy(out_hbm, w_out, sems.at[1])
    load_in.start()
    load_out.start()
    mark_ref[...] = jnp.zeros_like(mark_ref)
    core = lax.axis_index("core")
    n = w_in.shape[1] // 2
    other, own = side_of(1 - core, chips, n), side_of(core, chips, n)
    load_in.wait()
    send_ref[0] = dot(w_in[...], other, 1, 1).astype(BF16)
    send_ref[1] = dot(w_in[...], own, 1, 1).astype(BF16)
    load_out.wait()
    send_ref[2] = dot(other, w_out[...], 1, 1).astype(BF16)


def keep_kernel(owners, rows, chips, out_hbm, gain_ref, ids_ref, keep_ref, gains_ref, slot_ref, w_out, sems):
    load = pltpu.make_async_copy(out_hbm, w_out, sems.at[0])
    load.start()
    owner, _, rank, _ = ranked(ids_ref[...], owners, rows)
    slot_ref[...] = owner * SLOTS + rank
    core = lax.axis_index("core")
    feats = w_out.shape[1]
    block = feats // (2 * chips)
    gain = jnp.transpose(jnp.broadcast_to(gain_ref[...].reshape(1, feats), (8, feats)))[:, :1]
    for i in range(chips):
        for j in range(2):
            at = (2 * i + j) * block
            gains_ref[jnp.where(core == j, 0, 1), pl.ds(i * block, block), :] = gain[at:at + block]
    pick = side_of(core, chips, feats // 2)
    load.wait()
    keep_ref[...] = dot(pick, w_out[...], 1, 1).astype(BF16)


def rows_kernel(block_ref, table_hbm, _, out_ref, table, sems):
    load = pltpu.make_async_copy(table_hbm, table, sems.at[0])
    load.start()
    sources = block_ref.shape[0]
    feats, rows = table.shape
    n = sources * TALL
    code = block_ref[:, 0, :]
    spread = hot(iota((n, sources), 0) // TALL == iota((n, sources), 1))
    high = (code // SPLIT).astype(F32).astype(BF16)
    low = (code % SPLIT).astype(F32).astype(BF16)
    wide = dot(spread, high, 1, 0) * SPLIT + dot(spread, low, 1, 0)
    row, slot = iota((n, SLOTS), 0) % TALL, iota((n, SLOTS), 1)
    lane = iota((n, rows), 1)
    picks = []
    for j in range(WIDE):
        local = jnp.sum(jnp.where(slot == row * WIDE + j, wide, 0.0), axis=1, keepdims=True).astype(I32) - 1
        picks.append(hot(lane == local))
    out_ref[...] = jnp.zeros_like(out_ref)
    load.wait()
    for j, pick in enumerate(picks):
        x = dot(pick, table[...], 1, 1)
        out_ref[:, :, j * LANES:j * LANES + feats] = x.reshape(sources, TALL, feats).astype(BF16)


def scaled_of(x_ref, gain):
    chips, step, cols = x_ref.shape
    x = x_ref[...].reshape(chips * step, cols).astype(F32)
    return (gain * x).astype(BF16), jnp.sum(x * x, axis=0, keepdims=True)


def first_kernel(x_ref, gains_ref, mine_ref, other_ref, pre_ref, square_ref):
    scaled, square_ref[...] = scaled_of(x_ref, gains_ref[0])
    pre_ref[0] = dot(mine_ref[1], scaled, 1, 0)
    pre_ref[1] = dot(other_ref[0], scaled, 1, 0)


def second_kernel(x_ref, gains_ref, mine_ref, other_ref, keep_ref, pre_ref, square_ref, out_ref, hidden):
    scaled, squares = scaled_of(x_ref, gains_ref[1])
    squares += square_ref[...]
    scale = lax.rsqrt(squares / (2 * scaled.shape[0]) + NORM_EPS)
    for i, w in enumerate((mine_ref[0], other_ref[1])):
        pre = (pre_ref[i] + dot(w, scaled, 1, 0)) * scale
        hidden[i] = jax.nn.gelu(pre, approximate=True).astype(BF16)
    total = dot(keep_ref[...], hidden[0], 1, 0) + dot(other_ref[2], hidden[1], 1, 0)
    out_ref[...] = total.astype(BF16).reshape(out_ref.shape)


def place_kernel(back_ref, slot_ref, x_ref):
    chips, feats, toks = x_ref.shape
    n = back_ref.shape[0] * TALL
    slot = slot_ref[...]
    owner, rank = slot // SLOTS, slot % SLOTS
    x = jnp.zeros((feats, toks), F32)
    for j in range(WIDE):
        back = back_ref[:, :, j * LANES:j * LANES + feats].astype(F32).reshape(n, feats).astype(BF16)
        at = jnp.where(rank % WIDE == j, owner * TALL + rank // WIDE, -1)
        x += dot(back, hot(iota((n, toks), 0) == at), 0, 0)
    x = x.astype(BF16)
    for i in range(chips):
        x_ref[i] = x


def finish_kernel(parts_ref, x_ref, out_ref):
    total = x_ref[lax.axis_index("x")].astype(F32)
    for i in range(parts_ref.shape[0]):
        total += parts_ref[i].astype(F32)
    out_ref[...] = total.astype(BF16)


def call(kernel, out_shape, scratch=(), vmem=32 * 1024 * 1024, flops=None, **more):
    return pl.pallas_call(
        kernel,
        out_shape=out_shape,
        scratch_shapes=list(scratch),
        cost_estimate=flops and pl.CostEstimate(flops=flops, bytes_accessed=0, transcendentals=0),
        compiler_params=pltpu.CompilerParams(vmem_limit_bytes=vmem),
        **more,
    )


def on_device(neighbour_ids, table_cols, gain, w_in, w_out):
    seq = ("y", "z")
    owners = lax.axis_size(seq)
    chips = lax.axis_size("x")
    feat_local, rows = table_cols.shape
    feats, half = w_in.shape
    toks = neighbour_ids.shape[0]
    shape = jax.ShapeDtypeStruct

    ids = neighbour_ids.reshape(1, toks)
    outgoing = call(functools.partial(request_kernel, rows), shape((owners, 1, SLOTS), I32))(ids)
    block = lax.all_to_all(outgoing, seq, split_axis=0, concat_axis=0, tiled=True)
    swap = [(0, 1), (1, 0)]
    anywhere, vmem = pl.BlockSpec(memory_space=pl.ANY), pl.BlockSpec(memory_space=pltpu.VMEM)
    w_in_t = w_in.T
    w_send, mark = call(
        functools.partial(send_kernel, chips),
        (shape((3, half, half), BF16), shape((8, 128), I32)),
        (pltpu.VMEM((half, feats), BF16), pltpu.VMEM((half, feats), BF16), pltpu.SemaphoreType.DMA((2,))),
        in_specs=[anywhere, anywhere],
        vmem=60_000_000,
    )(w_in_t, w_out)
    asked = call(
        rows_kernel,
        shape((owners, TALL, WIDE * LANES), BF16),
        (pltpu.VMEM((feat_local, rows), BF16), pltpu.SemaphoreType.DMA((1,))),
        in_specs=[vmem, anywhere, anywhere],
        flops=10_000_000_000,
    )(block, table_cols, mark)
    back = lax.all_to_all(asked, seq, split_axis=0, concat_axis=0, tiled=True)
    w_later, gain_later, _ = lax.optimization_barrier((w_send, gain, block))
    w_other = lax.ppermute(w_later, "core", swap)
    w_keep, gains, slot = call(
        functools.partial(keep_kernel, owners, rows, chips),
        (shape((half, half), BF16), shape((2, half, 1), F32), shape((1, toks), I32)),
        (pltpu.VMEM((half, feats), BF16), pltpu.SemaphoreType.DMA((1,))),
        in_specs=[anywhere, vmem, vmem],
        vmem=32_000_000,
    )(w_out, gain_later, ids)
    spread = call(place_kernel, shape((chips, feat_local, toks), BF16), flops=10_000_000_000)(back, slot)
    x_mine = lax.all_to_all(spread, "x", split_axis=0, concat_axis=0, tiled=True)
    x_other = lax.ppermute(x_mine, "core", swap)
    pre, square = call(first_kernel, (shape((2, half, toks), F32), shape((1, toks), F32)))(
        x_mine, gains, w_send, w_other
    )
    parts = call(second_kernel, shape((chips, feat_local, toks), BF16), (pltpu.VMEM((2, half, toks), BF16),))(
        x_other, gains, w_send, w_other, w_keep, pre, square
    )
    parts = lax.all_to_all(parts, "x", split_axis=0, concat_axis=0, tiled=True)
    return call(finish_kernel, shape((feat_local, toks), BF16))(parts, x_mine)


def solution(mesh):
    fine = Mesh(mesh.devices.reshape(8, 12, 4, 2), ("y", "z", "x", "core"))
    seq, vocab = ("y", "z"), ("x", "core")
    in_specs = (P(seq), P(vocab, seq), P(), P(None, vocab), P(vocab, None))
    return jax.shard_map(
        on_device, mesh=fine, in_specs=in_specs, out_specs=P(vocab, seq), check_vma=False
    )
```

```python
import functools

import jax
import jax.numpy as jnp
from jax import lax
from jax.experimental import pallas as pl
from jax.experimental.pallas import tpu as pltpu
from jax.sharding import Mesh, PartitionSpec as P

TALL, WIDE, LANES = 2, 3, 128
SLOTS = 8
SPLIT = 64
NORM_EPS = 1e-05
F32 = jnp.float32
BF16 = jnp.bfloat16
I32 = jnp.int32


def iota(shape, dim):
    return lax.broadcasted_iota(I32, shape, dim)


def hot(mask):
    return jnp.where(mask, 1.0, 0.0).astype(BF16)


def dot(a, b, ca, cb):
    return lax.dot_general(a, b, (((ca,), (cb,)), ((), ())), preferred_element_type=F32)


def ranked(ids, owners, rows):
    toks = ids.shape[1]
    owner = ids // rows
    mine = iota((owners, toks), 0) == owner
    mine_hot = hot(mine)
    earlier = hot(iota((toks, toks), 0) < iota((toks, toks), 1))
    count = dot(mine_hot, earlier, 1, 0)
    rank = jnp.sum(jnp.where(mine, count, 0.0), axis=0, keepdims=True).astype(I32)
    return owner, ids - owner * rows + 1, rank, mine_hot


def request_kernel(rows, ids_ref, out_ref):
    owner, code, rank, mine_hot = ranked(ids_ref[...], out_ref.shape[0], rows)
    at = iota((SLOTS, ids_ref.shape[1]), 0) == rank
    high = jnp.where(at, code // SPLIT, 0).astype(F32).astype(BF16)
    low = jnp.where(at, code % SPLIT, 0).astype(F32).astype(BF16)
    out = dot(mine_hot, high, 1, 1) * SPLIT + dot(mine_hot, low, 1, 1)
    out_ref[:, 0, :] = out.astype(I32)


def third(r, block, count):
    return sum((r >= k * block).astype(I32) for k in range(1, count))


def blocks_kernel(owners, rows, chips, w_ref, ids_ref, keep_ref, send_ref, slot_ref, mark_ref):
    mark_ref[...] = jnp.zeros_like(mark_ref)
    owner, _, rank, _ = ranked(ids_ref[...], owners, rows)
    slot_ref[...] = owner * SLOTS + rank
    feats = w_ref.shape[1]
    n = feats // 2
    block = n // chips
    core = lax.axis_index("core")
    row, lane = iota((n, feats), 0), iota((n, feats), 1)
    base = row + third(row, block, chips) * block
    send_ref[...] = dot(hot(lane == base + (1 - core) * block), w_ref[...], 1, 1).astype(BF16)
    keep_ref[...] = dot(hot(lane == base + core * block), w_ref[...], 1, 1).astype(BF16)


def rows_kernel(block_ref, table_ref, _, out_ref, pick):
    sources = block_ref.shape[0]
    feats, rows = table_ref.shape
    n = sources * TALL
    code = block_ref[:, 0, :]
    spread = hot(iota((n, sources), 0) // TALL == iota((n, sources), 1))
    high = (code // SPLIT).astype(F32).astype(BF16)
    low = (code % SPLIT).astype(F32).astype(BF16)
    wide = dot(spread, high, 1, 0) * SPLIT + dot(spread, low, 1, 0)
    row, slot = iota((n, SLOTS), 0) % TALL, iota((n, SLOTS), 1)
    lane = iota((n, rows), 1)
    for j in range(WIDE):
        local = jnp.sum(jnp.where(slot == row * WIDE + j, wide, 0.0), axis=1, keepdims=True).astype(I32) - 1
        pick[j * n:(j + 1) * n] = hot(lane == local)
    out_ref[...] = jnp.zeros_like(out_ref)
    x = dot(pick[...], table_ref[...], 1, 1)
    for j in range(WIDE):
        out_ref[:, :, j * LANES:j * LANES + feats] = x[j * n:(j + 1) * n].reshape(sources, TALL, feats).astype(BF16)


def layer_kernel(x_ref, gain_ref, in_a, in_b, out_a, out_b, part_ref):
    feats = gain_ref.shape[0]
    x = x_ref[...].reshape(feats, x_ref.shape[2]).astype(F32)
    gain = jnp.transpose(jnp.broadcast_to(gain_ref[...].reshape(1, feats), (8, feats)))[:, :1]
    scaled = (gain * x).astype(BF16)
    scale = lax.rsqrt(jnp.sum(x * x, axis=0, keepdims=True) / feats + NORM_EPS)
    total = 0.0
    for w_in, w_out in ((in_a, out_a), (in_b, out_b)):
        pre = dot(w_in[...], scaled, 1, 0) * scale
        hidden = jax.nn.gelu(pre, approximate=True).astype(BF16)
        total += dot(w_out[...], hidden, 1, 0)
    part_ref[...] = total.astype(BF16).reshape(part_ref.shape)


def place_kernel(back_ref, slot_ref, x_ref):
    copies, feats, toks = x_ref.shape
    n = back_ref.shape[0] * TALL
    slot = slot_ref[...]
    owner, rank = slot // SLOTS, slot % SLOTS
    x = jnp.zeros((feats, toks), F32)
    for j in range(WIDE):
        back = back_ref[:, :, j * LANES:j * LANES + feats].astype(F32).reshape(n, feats).astype(BF16)
        at = jnp.where(rank % WIDE == j, owner * TALL + rank // WIDE, -1)
        x += dot(back, hot(iota((n, toks), 0) == at), 0, 0)
    x = x.astype(BF16)
    for i in range(copies):
        x_ref[i] = x


def finish_kernel(parts_ref, x_ref, out_ref):
    total = x_ref[2 * lax.axis_index("x") + lax.axis_index("core")].astype(F32)
    for i in range(parts_ref.shape[0]):
        total += parts_ref[i].astype(F32)
    out_ref[...] = total.astype(BF16)


def call(kernel, out_shape, scratch=(), vmem=32 * 1024 * 1024, flops=None, **more):
    return pl.pallas_call(
        kernel,
        out_shape=out_shape,
        scratch_shapes=list(scratch),
        cost_estimate=flops and pl.CostEstimate(flops=flops, bytes_accessed=0, transcendentals=0),
        compiler_params=pltpu.CompilerParams(vmem_limit_bytes=vmem),
        **more,
    )


def on_device(neighbour_ids, table_cols, gain, w_in, w_out):
    seq = ("y", "z")
    owners = lax.axis_size(seq)
    chips = lax.axis_size("x")
    feat_local, rows = table_cols.shape
    feats, half = w_in.shape
    toks = neighbour_ids.shape[0]
    shape = jax.ShapeDtypeStruct

    ids = neighbour_ids.reshape(1, toks)
    outgoing = call(functools.partial(request_kernel, rows), shape((owners, 1, SLOTS), I32))(ids)
    block = lax.all_to_all(outgoing, seq, split_axis=0, concat_axis=0, tiled=True)
    swap = [(0, 1), (1, 0)]
    anywhere, vmem = pl.BlockSpec(memory_space=pl.ANY), pl.BlockSpec(memory_space=pltpu.VMEM)
    out_own, out_send, slot, mark = call(
        functools.partial(blocks_kernel, owners, rows, chips),
        (shape((feats // 2, half), BF16),) * 2 + (shape((1, toks), I32), shape((8, 128), I32)),
    )(w_out, ids)
    asked = call(
        rows_kernel,
        shape((owners, TALL, WIDE * LANES), BF16),
        (pltpu.VMEM((owners * TALL * WIDE, rows), BF16),),
        in_specs=[vmem, vmem, anywhere],
        flops=10_000_000_000,
    )(block, table_cols, mark)
    back = lax.all_to_all(asked, seq, split_axis=0, concat_axis=0, tiled=True)
    in_own = w_in.T
    in_later, out_later, _ = lax.optimization_barrier((in_own, out_send, block))
    in_other = lax.ppermute(in_later, "core", swap)
    out_other = lax.ppermute(out_later, "core", swap)
    spread = call(place_kernel, shape((2 * chips, feat_local, toks), BF16), flops=10_000_000_000)(back, slot)
    spread, in_other, out_other = lax.optimization_barrier((spread, in_other, out_other))
    x = lax.all_to_all(spread, ("x", "core"), split_axis=0, concat_axis=0, tiled=True)
    parts = call(layer_kernel, shape((chips, feat_local, toks), BF16))(
        x, gain, in_own, in_other, out_own, out_other
    )
    parts = lax.all_to_all(parts, "x", split_axis=0, concat_axis=0, tiled=True)
    return call(finish_kernel, shape((feat_local, toks), BF16))(parts, x)


def solution(mesh):
    fine = Mesh(mesh.devices.reshape(8, 12, 4, 2), ("y", "z", "x", "core"))
    seq, vocab = ("y", "z"), ("x", "core")
    in_specs = (P(seq), P(vocab, seq), P(), P(None, vocab), P(vocab, None))
    return jax.shard_map(
        on_device, mesh=fine, in_specs=in_specs, out_specs=P(vocab, seq), check_vma=False
    )
```

```python
import functools

import jax
import jax.numpy as jnp
from jax import lax
from jax.experimental import pallas as pl
from jax.experimental.pallas import tpu as pltpu
from jax.sharding import Mesh, PartitionSpec as P

TALL, WIDE, LANES = 2, 3, 128
SLOTS = 8
SPLIT = 64
NORM_EPS = 1e-05
F32 = jnp.float32
BF16 = jnp.bfloat16
I32 = jnp.int32


def iota(shape, dim):
    return lax.broadcasted_iota(I32, shape, dim)


def hot(mask):
    return jnp.where(mask, 1.0, 0.0).astype(BF16)


def dot(a, b, ca, cb):
    return lax.dot_general(a, b, (((ca,), (cb,)), ((), ())), preferred_element_type=F32)


def ranked(ids, owners, rows):
    toks = ids.shape[1]
    owner = ids // rows
    mine = iota((owners, toks), 0) == owner
    mine_hot = hot(mine)
    earlier = hot(iota((toks, toks), 0) < iota((toks, toks), 1))
    count = dot(mine_hot, earlier, 1, 0)
    rank = jnp.sum(jnp.where(mine, count, 0.0), axis=0, keepdims=True).astype(I32)
    return owner, ids - owner * rows + 1, rank, mine_hot


def request_kernel(rows, ids_ref, out_ref):
    owner, code, rank, mine_hot = ranked(ids_ref[...], out_ref.shape[0], rows)
    at = iota((SLOTS, ids_ref.shape[1]), 0) == rank
    high = jnp.where(at, code // SPLIT, 0).astype(F32).astype(BF16)
    low = jnp.where(at, code % SPLIT, 0).astype(F32).astype(BF16)
    out = dot(mine_hot, high, 1, 1) * SPLIT + dot(mine_hot, low, 1, 1)
    out_ref[:, 0, :] = out.astype(I32)


def slot_kernel(owners, rows, ids_ref, slot_ref):
    owner, _, rank, _ = ranked(ids_ref[...], owners, rows)
    slot_ref[...] = owner * SLOTS + rank


def rows_kernel(block_ref, table_ref, out_ref, pick):
    sources = block_ref.shape[0]
    feats, rows = table_ref.shape
    n = sources * TALL
    code = block_ref[:, 0, :]
    spread = hot(iota((n, sources), 0) // TALL == iota((n, sources), 1))
    high = (code // SPLIT).astype(F32).astype(BF16)
    low = (code % SPLIT).astype(F32).astype(BF16)
    wide = dot(spread, high, 1, 0) * SPLIT + dot(spread, low, 1, 0)
    row, slot = iota((n, SLOTS), 0) % TALL, iota((n, SLOTS), 1)
    lane = iota((n, rows), 1)
    for j in range(WIDE):
        local = jnp.sum(jnp.where(slot == row * WIDE + j, wide, 0.0), axis=1, keepdims=True).astype(I32) - 1
        pick[j * n:(j + 1) * n] = hot(lane == local)
    out_ref[...] = jnp.zeros_like(out_ref)
    x = dot(pick[...], table_ref[...], 1, 1)
    for j in range(WIDE):
        out_ref[:, :, j * LANES:j * LANES + feats] = x[j * n:(j + 1) * n].reshape(sources, TALL, feats).astype(BF16)


def layer_kernel(x_ref, gain_ref, in_a, out_a, in_b, out_b, part_ref):
    feats = in_a.shape[1]
    x = x_ref[...].reshape(feats, x_ref.shape[2]).astype(F32)
    gain = jnp.transpose(jnp.broadcast_to(gain_ref[...].reshape(1, feats), (8, feats)))[:, :1]
    scaled = (gain * x).astype(BF16)
    scale = lax.rsqrt(jnp.sum(x * x, axis=0, keepdims=True) / feats + NORM_EPS)
    total = 0.0
    for w_in, w_out in ((in_a, out_a), (in_b, out_b)):
        pre = dot(w_in[...], scaled, 1, 0) * scale
        hidden = jax.nn.gelu(pre, approximate=True).astype(BF16)
        total += dot(hidden, w_out[...], 0, 0)
    part_ref[...] = jnp.transpose(total).astype(BF16).reshape(part_ref.shape)


def place_kernel(back_ref, slot_ref, x_ref, own_ref):
    feats, toks = own_ref.shape
    n = back_ref.shape[0] * TALL
    slot = slot_ref[...]
    owner, rank = slot // SLOTS, slot % SLOTS
    x = jnp.zeros((feats, toks), F32)
    for j in range(WIDE):
        back = back_ref[:, :, j * LANES:j * LANES + feats].astype(F32).reshape(n, feats).astype(BF16)
        at = jnp.where(rank % WIDE == j, owner * TALL + rank // WIDE, -1)
        x += dot(back, hot(iota((n, toks), 0) == at), 0, 0)
    x = x.astype(BF16)
    own_ref[...] = x
    part = toks // 2
    for i in range(x_ref.shape[0]):
        x_ref[i] = x[:, i % 2 * part:(i % 2 + 1) * part]


def finish_kernel(parts_ref, own_ref, out_ref):
    part = parts_ref.shape[2]
    for core in range(2):
        at = slice(core * part, (core + 1) * part)
        total = own_ref[:, at].astype(F32)
        for i in range(core, parts_ref.shape[0], 2):
            total += parts_ref[i].astype(F32)
        out_ref[:, at] = total.astype(BF16)


def call(kernel, out_shape, scratch=(), vmem=32 * 1024 * 1024, flops=None, **more):
    return pl.pallas_call(
        kernel,
        out_shape=out_shape,
        scratch_shapes=list(scratch),
        cost_estimate=flops and pl.CostEstimate(flops=flops, bytes_accessed=0, transcendentals=0),
        compiler_params=pltpu.CompilerParams(vmem_limit_bytes=vmem),
        **more,
    )


def on_device(neighbour_ids, table_cols, gain, w_in, w_out):
    seq = ("y", "z")
    owners = lax.axis_size(seq)
    vocab = 2 * lax.axis_size("x")
    feat_local, rows = table_cols.shape
    feats, half = w_in.shape
    toks = neighbour_ids.shape[0]
    shape = jax.ShapeDtypeStruct

    ids = neighbour_ids.reshape(1, toks)
    outgoing = call(functools.partial(request_kernel, rows), shape((owners, 1, SLOTS), I32))(ids)
    block = lax.all_to_all(outgoing, seq, split_axis=0, concat_axis=0, tiled=True)
    swap = [(0, 1), (1, 0)]
    slot = call(functools.partial(slot_kernel, owners, rows), shape((1, toks), I32))(ids)
    asked = call(
        rows_kernel,
        shape((owners, TALL, WIDE * LANES), BF16),
        (pltpu.VMEM((owners * TALL * WIDE, rows), BF16),),
        flops=10_000_000_000,
    )(block, table_cols)
    back = lax.all_to_all(asked, seq, split_axis=0, concat_axis=0, tiled=True)
    weights = w_in.T, w_out
    others = [lax.ppermute(w, "core", swap) for w in weights]
    spread, own = call(
        place_kernel,
        (shape((vocab, feat_local, toks // 2), BF16), shape((feat_local, toks), BF16)),
        flops=10_000_000_000,
    )(back, slot)
    spread, others = lax.optimization_barrier((spread, others))
    x = lax.all_to_all(spread, ("x", "core"), split_axis=0, concat_axis=0, tiled=True)
    parts = call(layer_kernel, shape((vocab, feat_local, toks // 2), BF16))(
        x, gain, *weights, *others
    )
    parts = lax.all_to_all(parts, ("x", "core"), split_axis=0, concat_axis=0, tiled=True)
    return call(finish_kernel, shape((feat_local, toks), BF16))(parts, own)


def solution(mesh):
    fine = Mesh(mesh.devices.reshape(8, 12, 4, 2), ("y", "z", "x", "core"))
    seq, vocab = ("y", "z"), ("x", "core")
    in_specs = (P(seq), P(vocab, seq), P(), P(None, vocab), P(vocab, None))
    return jax.shard_map(
        on_device, mesh=fine, in_specs=in_specs, out_specs=P(vocab, seq), check_vma=False
    )
```

```python
import functools

import jax
import jax.numpy as jnp
from jax import lax
from jax.experimental import pallas as pl
from jax.experimental.pallas import tpu as pltpu
from jax.sharding import Mesh, PartitionSpec as P

TALL, WIDE, LANES = 2, 3, 128
SLOTS = 8
SPLIT = 64
NORM_EPS = 1e-05
F32 = jnp.float32
BF16 = jnp.bfloat16
I32 = jnp.int32


def iota(shape, dim):
    return lax.broadcasted_iota(I32, shape, dim)


def hot(mask):
    return jnp.where(mask, 1.0, 0.0).astype(BF16)


def dot(a, b, ca, cb):
    return lax.dot_general(a, b, (((ca,), (cb,)), ((), ())), preferred_element_type=F32)


def ranked(ids, owners, rows):
    toks = ids.shape[1]
    owner = ids // rows
    mine = iota((owners, toks), 0) == owner
    mine_hot = hot(mine)
    earlier = hot(iota((toks, toks), 0) < iota((toks, toks), 1))
    count = dot(mine_hot, earlier, 1, 0)
    rank = jnp.sum(jnp.where(mine, count, 0.0), axis=0, keepdims=True).astype(I32)
    return owner, ids - owner * rows + 1, rank, mine_hot


def request_kernel(rows, ids_ref, out_ref):
    owner, code, rank, mine_hot = ranked(ids_ref[...], out_ref.shape[0], rows)
    at = iota((SLOTS, ids_ref.shape[1]), 0) == rank
    high = jnp.where(at, code // SPLIT, 0).astype(F32).astype(BF16)
    low = jnp.where(at, code % SPLIT, 0).astype(F32).astype(BF16)
    out = dot(mine_hot, high, 1, 1) * SPLIT + dot(mine_hot, low, 1, 1)
    out_ref[:, 0, :] = out.astype(I32)


def slot_kernel(owners, rows, ids_ref, slot_ref):
    owner, _, rank, _ = ranked(ids_ref[...], owners, rows)
    slot_ref[...] = owner * SLOTS + rank


def rows_kernel(block_ref, table_ref, out_ref, pick, sides):
    sources = block_ref.shape[0]
    feats, rows = table_ref.shape
    part = rows // 2
    n = sources * TALL
    sides[...] = jnp.zeros_like(sides)
    for i in range(2):
        sides[i * LANES:i * LANES + feats] = table_ref[:, i * part:(i + 1) * part]
    code = block_ref[:, 0, :]
    spread = hot(iota((n, sources), 0) // TALL == iota((n, sources), 1))
    high = (code // SPLIT).astype(F32).astype(BF16)
    low = (code % SPLIT).astype(F32).astype(BF16)
    wide = dot(spread, high, 1, 0) * SPLIT + dot(spread, low, 1, 0)
    row, slot = iota((n, SLOTS), 0) % TALL, iota((n, SLOTS), 1)
    lane = iota((n, part), 1)
    later = []
    for j in range(WIDE):
        local = jnp.sum(jnp.where(slot == row * WIDE + j, wide, 0.0), axis=1, keepdims=True).astype(I32) - 1
        later.append(local >= part)
        pick[j * n:(j + 1) * n] = hot(lane == jnp.where(later[j], local - part, local))
    out_ref[...] = jnp.zeros_like(out_ref)
    x = dot(pick[...], sides[...], 1, 1)
    for j in range(WIDE):
        mine = x[j * n:(j + 1) * n]
        mine = jnp.where(later[j], mine[:, LANES:LANES + feats], mine[:, :feats])
        out_ref[:, :, j * LANES:j * LANES + feats] = mine.reshape(sources, TALL, feats).astype(BF16)


def layer_kernel(x_ref, gain_ref, in_a, out_a, in_b, out_b, part_ref):
    feats = in_a.shape[1]
    x = x_ref[...].reshape(feats, x_ref.shape[2]).astype(F32)
    gain = jnp.transpose(jnp.broadcast_to(gain_ref[...].reshape(1, feats), (8, feats)))[:, :1]
    scaled = (gain * x).astype(BF16)
    scale = lax.rsqrt(jnp.sum(x * x, axis=0, keepdims=True) / feats + NORM_EPS)
    total = 0.0
    for w_in, w_out in ((in_a, out_a), (in_b, out_b)):
        pre = dot(w_in[...], scaled, 1, 0) * scale
        hidden = jax.nn.gelu(pre, approximate=True).astype(BF16)
        total += dot(hidden, w_out[...], 0, 0)
    part_ref[...] = jnp.transpose(total).astype(BF16).reshape(part_ref.shape)


def place_kernel(back_ref, slot_ref, x_ref, own_ref):
    feats, toks = own_ref.shape
    n = back_ref.shape[0] * TALL
    slot = slot_ref[...]
    owner, rank = slot // SLOTS, slot % SLOTS
    x = jnp.zeros((feats, toks), F32)
    for j in range(WIDE):
        back = back_ref[:, :, j * LANES:j * LANES + feats].astype(F32).reshape(n, feats).astype(BF16)
        at = jnp.where(rank % WIDE == j, owner * TALL + rank // WIDE, -1)
        x += dot(back, hot(iota((n, toks), 0) == at), 0, 0)
    x = x.astype(BF16)
    own_ref[...] = x
    part = toks // 2
    for i in range(x_ref.shape[0]):
        x_ref[i] = x[:, i % 2 * part:(i % 2 + 1) * part]


def finish_kernel(parts_ref, own_ref, out_ref):
    part = parts_ref.shape[2]
    for core in range(2):
        at = slice(core * part, (core + 1) * part)
        total = own_ref[:, at].astype(F32)
        for i in range(core, parts_ref.shape[0], 2):
            total += parts_ref[i].astype(F32)
        out_ref[:, at] = total.astype(BF16)


def call(kernel, out_shape, scratch=(), vmem=32 * 1024 * 1024, flops=None, **more):
    return pl.pallas_call(
        kernel,
        out_shape=out_shape,
        scratch_shapes=list(scratch),
        cost_estimate=flops and pl.CostEstimate(flops=flops, bytes_accessed=0, transcendentals=0),
        compiler_params=pltpu.CompilerParams(vmem_limit_bytes=vmem),
        **more,
    )


def on_device(neighbour_ids, table_cols, gain, w_in, w_out):
    seq = ("y", "z")
    owners = lax.axis_size(seq)
    vocab = 2 * lax.axis_size("x")
    feat_local, rows = table_cols.shape
    feats, half = w_in.shape
    toks = neighbour_ids.shape[0]
    shape = jax.ShapeDtypeStruct

    ids = neighbour_ids.reshape(1, toks)
    outgoing = call(functools.partial(request_kernel, rows), shape((owners, 1, SLOTS), I32))(ids)
    block = lax.all_to_all(outgoing, seq, split_axis=0, concat_axis=0, tiled=True)
    swap = [(0, 1), (1, 0)]
    slot = call(functools.partial(slot_kernel, owners, rows), shape((1, toks), I32))(ids)
    asked = call(
        rows_kernel,
        shape((owners, TALL, WIDE * LANES), BF16),
        (pltpu.VMEM((owners * TALL * WIDE, rows // 2), BF16), pltpu.VMEM((2 * LANES, rows // 2), BF16)),
        flops=10_000_000_000,
    )(block, table_cols)
    back = lax.all_to_all(asked, seq, split_axis=0, concat_axis=0, tiled=True)
    weights = w_in.T, w_out
    others = [lax.ppermute(w, "core", swap) for w in weights]
    spread, own = call(
        place_kernel,
        (shape((vocab, feat_local, toks // 2), BF16), shape((feat_local, toks), BF16)),
        flops=10_000_000_000,
    )(back, slot)
    spread, others = lax.optimization_barrier((spread, others))
    x = lax.all_to_all(spread, ("x", "core"), split_axis=0, concat_axis=0, tiled=True)
    parts = call(layer_kernel, shape((vocab, feat_local, toks // 2), BF16))(
        x, gain, *weights, *others
    )
    parts = lax.all_to_all(parts, ("x", "core"), split_axis=0, concat_axis=0, tiled=True)
    return call(finish_kernel, shape((feat_local, toks), BF16))(parts, own)


def solution(mesh):
    fine = Mesh(mesh.devices.reshape(8, 12, 4, 2), ("y", "z", "x", "core"))
    seq, vocab = ("y", "z"), ("x", "core")
    in_specs = (P(seq), P(vocab, seq), P(), P(None, vocab), P(vocab, None))
    return jax.shard_map(
        on_device, mesh=fine, in_specs=in_specs, out_specs=P(vocab, seq), check_vma=False
    )
```
